512 devices in a mesh: layer: 4 (over y), row: 8 (over x, core), col: 16 (over z).
Axes of the slice: x: 4, y: 4, z: 16, core: 2. Of those that a mesh axis runs over, the one named last changes fastest.
Arguments:
- stiff_blocks: bfloat16 [4, 8, 16, 2, 16, 4096], P('layer', 'row', 'col'), may hold values from -0.19921875 to 0.19921875
- block_pos: int32 [4, 8, 16, 2, 16], P('layer', 'row', 'col'), may hold values from 0 to 31, as said below
- block_count: int32 [4, 8, 16, 2], P('layer', 'row', 'col'), may hold values from 4 to 16
- modes: bfloat16 [4, 2, 4096, 2048], P('layer', None, 'row', 'col'), may hold values from -6 to 6
- panel_owner: int32 [4, 2, 64], P('layer'), may hold values from 0 to 63, each once within a row
Outputs:
- stiff_modes: bfloat16 [4096, 2048], P(('row', 'layer'), 'col')
The draws below stay inside these ranges and needn't reach their ends.
Inputs may be any that keep to these rules, and one draw needn't show every extreme that they name: `block_pos`: the positions of one piece are all different.
All inputs are finite; a program needn't handle non-finite values.
Results may differ from the reference program's by a relative error of at most 0.011.
Values may be sent and summed in bfloat16 or wider, within the bound.
No kernel may reach another device: no remote copies, remote signals or barrier semaphores. Data moves between devices by JAX's collectives and lax.ppermute only.
A program may use at most 128 MiB of HBM per device.

```python
import jax
import jax.numpy as jnp
from jax import lax

BLK = 64
KW = 4
STEPS = 2
BR_DEV = 8
NC = 128
NNZ = 16
KB = 8
PBLK = 64
MODES = 2048
N_LAYER = 4
N_ROW = 8
N_COL = 16


def draw_block_pos(key, part):
    key = jax.random.fold_in(key, 11)
    count = N_LAYER * N_ROW * N_COL * STEPS
    keys = jax.random.split(key, count)
    orders = jax.vmap(lambda k: jax.random.permutation(k, BR_DEV * KW))(keys)
    return orders[:, :NNZ].astype(jnp.int32).reshape(N_LAYER, N_ROW, N_COL, STEPS, NNZ)


def draw_block_count(key, part):
    key = jax.random.fold_in(key, 23)
    counts = jax.random.randint(key, (N_LAYER, N_ROW, N_COL, STEPS), NNZ // 4, NNZ + 1)
    counts = counts.at[0, 0, 0, 0].set(NNZ)
    return counts.astype(jnp.int32)


def block_scale(own_key, dims, shards, low, largest):
    level = 1.0
    for axis_at, blocks in shards:
        steps = jax.random.uniform(jax.random.fold_in(jax.random.fold_in(own_key, 6), axis_at), (blocks,), jnp.float32, low / len(shards), largest / len(shards))
        level = level * jnp.repeat(jnp.exp(steps), dims[axis_at] // blocks).reshape((-1,) + (1,) * (len(dims) - 1 - axis_at))
    return level


def scatter_about(own_key, dims, width, bound, cuts=(), kind=jnp.bfloat16):
    array = width * jax.random.normal(own_key, dims, jnp.float32)
    if cuts:
        array = array * block_scale(own_key, dims, cuts, -0.22, 0.18)
    return jnp.clip(array, -bound, bound).astype(kind)


def setup_inputs(seed: int = 0) -> dict:
    streams_of = jax.random.split(jax.random.key(seed), 6)
    stiff_blocks = scatter_about(streams_of[0], (N_LAYER, N_ROW, N_COL, STEPS, NNZ, BLK * BLK), 0.03, 0.19921875, ((0, 4), (1, 8), (2, 16)))
    block_pos = draw_block_pos(jax.random.fold_in(streams_of[5], 71), 0)
    block_count = draw_block_count(jax.random.fold_in(streams_of[5], 71), 0)
    modes = scatter_about(streams_of[3], (N_LAYER, STEPS, N_ROW * KB * BLK, MODES), 1.0, 6.0, ((0, 4), (2, 8), (3, 16)))
    panel_owner = jax.vmap(lambda own: jax.random.permutation(own, PBLK))(jax.random.split(streams_of[4], N_LAYER * STEPS)).reshape((N_LAYER, STEPS, PBLK)).astype(jnp.int32)
    return {"stiff_blocks": stiff_blocks, "block_pos": block_pos, "block_count": block_count, "modes": modes, "panel_owner": panel_owner}


def reference(stiff_blocks, block_pos, block_count, modes, panel_owner):
    total = jnp.zeros((N_ROW * BR_DEV * BLK, N_COL * NC), jnp.float32)
    slot_ids = jnp.arange(NNZ, dtype=jnp.int32)
    row_ids = jnp.arange(BR_DEV, dtype=jnp.int32)
    for layer in range(N_LAYER):
        for step in range(STEPS):
            panel = modes[layer, step].reshape(PBLK, BLK, N_COL * NC)
            panel = jnp.take(panel, panel_owner[layer, step].astype(jnp.int32), axis=0)

            def one_row(packed):
                vals, pos, cnt = packed

                def one_piece(acc, inner):
                    piece_vals, piece_pos, piece_cnt, col_index = inner
                    live = slot_ids < piece_cnt
                    blocks = jnp.where(live[:, None], piece_vals, jnp.zeros_like(piece_vals))
                    blocks = blocks.astype(jnp.float32).reshape(NNZ, BLK, BLK)
                    target = col_index * KW + piece_pos % KW
                    met = jnp.take(panel, target.astype(jnp.int32), axis=0).astype(jnp.float32)
                    prod = jnp.einsum("nab,nbc->nac", blocks, met)
                    onehot = (row_ids[:, None] == (piece_pos // KW)[None, :]).astype(jnp.float32)
                    acc = acc + jnp.einsum("rn,nac->rac", onehot, prod).reshape(BR_DEV * BLK, N_COL * NC)
                    return acc, None

                start = jnp.zeros((BR_DEV * BLK, N_COL * NC), jnp.float32)
                cols = jnp.arange(N_COL, dtype=jnp.int32)
                acc, unused = lax.scan(one_piece, start, (vals, pos, cnt, cols))
                return acc

            parts = lax.map(one_row, (stiff_blocks[layer, :, :, step], block_pos[layer, :, :, step], block_count[layer, :, :, step]))
            total = total + parts.reshape(N_ROW * BR_DEV * BLK, N_COL * NC)
    return total.astype(jnp.bfloat16)
```

```python
import jax
import jax.numpy as jnp
from jax import lax
from jax.experimental import pallas as pl
from jax.experimental.pallas import tpu as pltpu
from jax.sharding import PartitionSpec as P

BLK = 64
KW = 4
STEPS = 2
LANES = 128
NCH = 4


def fill_rhs(rhs_ref, b_ref, own_ref, s, g0, row0, blks):
    for bc in range(KW):
        p = own_ref[s, g0 + bc]
        blk = b_ref[((p // blks) * STEPS + s) * blks + p % blks]
        for h in range(2):
            r = row0 + bc * LANES + h * BLK
            rhs_ref[r : r + BLK, h * LANES : (h + 1) * LANES] = blk


def fill_lhs(lhs_ref, raw, spot, col0, brows):
    slots = raw.shape[0]
    tiles = raw.shape[1] // LANES
    ids = lax.broadcasted_iota(jnp.int32, (KW * brows, slots), 0)
    onehot = jnp.where(ids == spot, 1.0, 0.0).astype(jnp.bfloat16)
    dense = jnp.dot(onehot, raw, preferred_element_type=jnp.float32)
    for bc in range(KW):
        cols = jnp.concatenate(
            [
                dense[bc * brows : (bc + 1) * brows, k * LANES : (k + 1) * LANES]
                for k in range(tiles)
            ],
            axis=0,
        )
        lhs_ref[:, col0 + bc * LANES : col0 + (bc + 1) * LANES] = cols.astype(jnp.bfloat16)


def product_kernel(own_ref, a_ref, spot_ref, b_ref, out_ref, lhs_ref, rhs_ref, acc_ref, *, brows, blks):
    step = pl.program_id(0)
    per = a_ref.shape[0]
    width = KW * LANES

    @pl.when(step == 0)
    def _():
        rhs_ref[...] = jnp.zeros_like(rhs_ref)
        acc_ref[...] = jnp.zeros_like(acc_ref)

    def one(i, carry):
        c = step * per + i
        for s in range(STEPS):
            fill_lhs(lhs_ref, a_ref[i, s], spot_ref[i, s : s + 1, :], s * width, brows)
            fill_rhs(rhs_ref, b_ref, own_ref, s, c * KW, s * width, blks)
        more = jnp.dot(lhs_ref[...], rhs_ref[...], preferred_element_type=jnp.float32)
        for h in range(2):
            acc_ref[h] += more[:, h * LANES : (h + 1) * LANES]
        return carry

    lax.fori_loop(0, per, one, 0)

    @pl.when(step == pl.num_programs(0) - 1)
    def _():
        layers = out_ref.shape[0]
        per_layer = brows // layers
        tiles = acc_ref.shape[1] // brows
        for l in range(layers):
            for j in range(per_layer):
                for h in range(2):
                    out_ref[l, j * tiles : (j + 1) * tiles, h * LANES : (h + 1) * LANES] = acc_ref[
                        h, pl.ds(l * per_layer + j, tiles, stride=brows), :
                    ]


def finish_kernel(parts_ref, out_ref, rows_ref):
    total = jnp.sum(parts_ref[...], axis=0)
    tiles = BLK // 2
    for j in range(total.shape[0] // tiles):
        for h in range(2):
            rows_ref[pl.ds(j * BLK + h, tiles, stride=2), :] = total[
                j * tiles : (j + 1) * tiles, h * LANES : (h + 1) * LANES
            ]
    out_ref[...] = rows_ref[...].astype(jnp.bfloat16)


def body(stiff_blocks, block_pos, block_count, modes, panel_owner):
    layers = lax.axis_size("layer")
    rows_n = lax.axis_size("row")
    cols_n = lax.axis_size("col")
    slots = stiff_blocks.shape[4]
    brows = slots * 2 // KW
    width = modes.shape[3]
    depth = modes.shape[2]
    blks = depth // BLK

    slot_ids = jnp.arange(slots, dtype=jnp.int32)
    live = slot_ids[None, :] < block_count[0, 0, 0][:, None]
    pos = block_pos[0, 0, 0]
    spot = jnp.where(live, (pos % KW) * brows + pos // KW, KW * brows)

    a = lax.all_gather(stiff_blocks[0, 0], "col", axis=0, tiled=True)
    spot = lax.all_gather(spot, "col", axis=0, tiled=False)

    flat = modes.reshape(STEPS * depth, width)
    cut = STEPS * depth // NCH
    parts = [
        lax.all_gather(flat[i * cut : (i + 1) * cut], "row", axis=0, tiled=False) for i in range(NCH)
    ]
    b = jnp.concatenate(parts, axis=1).reshape(rows_n * STEPS * blks, BLK, width)

    per = 4
    tiles = BLK * BLK // LANES
    parts = pl.pallas_call(
        lambda *refs: product_kernel(*refs, brows=brows, blks=blks),
        grid_spec=pltpu.PrefetchScalarGridSpec(
            num_scalar_prefetch=1,
            grid=(cols_n // per,),
            in_specs=[
                pl.BlockSpec((per, STEPS, slots, BLK * BLK), lambda i, o: (i, 0, 0, 0)),
                pl.BlockSpec((per, STEPS, slots), lambda i, o: (i, 0, 0)),
                pl.BlockSpec((rows_n * STEPS * blks, BLK, width), lambda i, o: (0, 0, 0)),
            ],
            out_specs=pl.BlockSpec((layers, brows * tiles // layers, 2 * LANES), lambda i, o: (0, 0, 0)),
            scratch_shapes=[
                pltpu.VMEM((brows * tiles, STEPS * KW * LANES), jnp.bfloat16),
                pltpu.VMEM((STEPS * KW * LANES, 2 * LANES), jnp.bfloat16),
                pltpu.VMEM((2, brows * tiles, LANES), jnp.float32),
            ],
        ),
        out_shape=jax.ShapeDtypeStruct((layers, brows * tiles // layers, 2 * LANES), jnp.float32),
        compiler_params=pltpu.CompilerParams(vmem_limit_bytes=40 * 1024 * 1024),
        name="product",
    )(panel_owner[0], a, spot, b)
    parts = lax.all_to_all(parts, "layer", 0, 0, tiled=True)
    return pl.pallas_call(
        finish_kernel,
        out_shape=jax.ShapeDtypeStruct((brows * BLK // layers, width), jnp.bfloat16),
        scratch_shapes=[pltpu.VMEM((brows * BLK // layers, width), jnp.float32)],
        name="finish",
    )(parts)


def solution(mesh):
    return jax.shard_map(
        body,
        mesh=mesh,
        in_specs=(
            P("layer", "row", "col", None, None, None),
            P("layer", "row", "col", None, None),
            P("layer", "row", "col", None),
            P("layer", None, "row", "col"),
            P("layer", None, None),
        ),
        out_specs=P(("row", "layer"), "col"),
        check_vma=False,
    )
```

```python
import functools

import jax
import jax.numpy as jnp
from jax import lax
from jax.experimental import pallas as pl
from jax.experimental.pallas import tpu as pltpu
from jax.sharding import Mesh, PartitionSpec as P

BLK = 64
KW = 4
STEPS = 2
LANES = 128
TILES = BLK * BLK // LANES
FLAT = BLK * BLK
GROUP = 2


def product_kernel(*refs, parts, brows, slots, blks, group, first, last):
    own_ref, num_ref = refs[0], refs[1]
    count = max(ref for part in parts for ref, _ in part) + 1
    piece_refs = refs[2 : 2 + count]
    rest = refs[2 + count :]
    b_refs, rest = rest[:2], rest[2:]
    if not first:
        acc_in, rest = rest[0], rest[1:]
    out_ref, stage_ref, hot_ref, lhs_ref, rhs_ref, b_ref, sem = rest[:7]
    acc_ref = rest[7] if last else out_ref
    n = len(parts)
    width = KW * LANES
    chunk = group * LANES
    per_b = b_ref.shape[0] // 2

    copies = [
        pltpu.make_async_copy(b_refs[e], b_ref.at[pl.ds(e * per_b, per_b)], sem.at[e]) for e in range(2)
    ]
    for copy in copies:
        copy.start()
    for i, part in enumerate(parts):
        for s in range(STEPS):
            ref, off = part[s]
            stage_ref[i, s] = piece_refs[ref][:, off : off + FLAT]
            ref, off = part[STEPS]
            spot = piece_refs[ref][:, off : off + LANES].astype(jnp.float32)[s : s + 1, :slots]
            ids = lax.broadcasted_iota(jnp.int32, (KW * brows, slots), 0).astype(jnp.float32)
            hot_ref[i, s] = jnp.where(ids == spot, 1.0, 0.0).astype(jnp.bfloat16)
    rhs_ref[...] = jnp.zeros_like(rhs_ref)
    if first:
        acc_ref[...] = jnp.zeros_like(acc_ref)
    else:
        acc_ref[...] = acc_in[...]
    x, core = num_ref[n], num_ref[n + 1]
    for copy in copies:
        copy.wait()

    def one(i, carry):
        g0 = num_ref[i] * KW
        for s in range(STEPS):
            dense = jnp.dot(hot_ref[i, s], stage_ref[i, s], preferred_element_type=jnp.float32)
            for bc in range(KW):
                cols = jnp.concatenate(
                    [
                        dense[bc * brows : (bc + 1) * brows, k * LANES : (k + 1) * LANES]
                        for k in range(TILES)
                    ],
                    axis=0,
                )
                lhs_ref[:, s * width + bc * LANES : s * width + (bc + 1) * LANES] = cols.astype(jnp.bfloat16)
                p = own_ref[s, g0 + bc]
                row = p // blks
                side = (row % 2 + core) % 2
                ahead = (row // 2 + 4 - x) % 4
                for j in range(group):
                    at = (((side * 4 + ahead) * group + j) * STEPS + s) * blks + p % blks
                    blk = b_ref[at]
                    for h in range(2):
                        r = s * width + bc * LANES + h * BLK
                        c = h * chunk + j * LANES
                        rhs_ref[r : r + BLK, c : c + LANES] = blk
        more = jnp.dot(lhs_ref[...], rhs_ref[...], preferred_element_type=jnp.float32)
        for q in range(2 * group):
            acc_ref[q] += more[:, q * LANES : (q + 1) * LANES]
        return carry

    lax.fori_loop(0, n, one, 0)

    if last:
        zc = num_ref[n + 2]
        per_layer = out_ref.shape[1] // TILES
        layers = brows // per_layer
        for l in range(layers):
            for j in range(group):
                to = l * group + (zc + j) % group
                for m in range(per_layer):
                    for h in range(2):
                        out_ref[to, m * TILES : (m + 1) * TILES, h * LANES : (h + 1) * LANES] = acc_ref[
                            h * group + j, pl.ds(l * per_layer + m, TILES, stride=brows), :
                        ]


def product(own, nums, pieces, parts, b, acc, *, brows, slots, blks, layers, last):
    group = GROUP
    n = len(parts)
    first = acc is None
    rows = brows * TILES
    sums = jax.ShapeDtypeStruct((2 * group, rows, LANES), jnp.float32)
    outs = jax.ShapeDtypeStruct((layers * group, rows // layers, 2 * LANES), jnp.float32)
    vmem = pl.BlockSpec(memory_space=pltpu.VMEM)
    smem = pl.BlockSpec(memory_space=pltpu.SMEM)
    scratch = [
        pltpu.VMEM((n, STEPS, slots, FLAT), jnp.bfloat16),
        pltpu.VMEM((n, STEPS, KW * brows, slots), jnp.bfloat16),
        pltpu.VMEM((rows, STEPS * KW * LANES), jnp.bfloat16),
        pltpu.VMEM((STEPS * KW * LANES, 2 * group * LANES), jnp.bfloat16),
        pltpu.VMEM((2 * b[0].shape[0], BLK, LANES), jnp.bfloat16),
        pltpu.SemaphoreType.DMA((2,)),
    ]
    if last:
        scratch.append(pltpu.VMEM(sums.shape, jnp.float32))
    macs = n * STEPS * KW * LANES * rows * 2 * group * LANES
    return pl.pallas_call(
        functools.partial(
            product_kernel, parts=parts, brows=brows, slots=slots, blks=blks, group=group, first=first, last=last
        ),
        in_specs=[smem, smem] + [vmem] * len(pieces) + [pl.BlockSpec(memory_space=pl.ANY)] * 2 + [vmem] * (not first),
        out_specs=vmem,
        scratch_shapes=scratch,
        out_shape=outs if last else sums,
        compiler_params=pltpu.CompilerParams(vmem_limit_bytes=48 * 1024 * 1024),
        cost_estimate=pl.CostEstimate(flops=2 * macs, bytes_accessed=8 << 20, transcendentals=0),
        name="product_last" if last else "product",
    )(own, nums, *pieces, *b, *([] if first else [acc]))


def pack_kernel(stiff_ref, pos_ref, count_ref, out_ref, row_ref, *, brows):
    steps, slots, flat = stiff_ref.shape
    for s in range(steps):
        out_ref[:, s * flat : (s + 1) * flat] = stiff_ref[s]
    row_ref[...] = jnp.zeros_like(row_ref)
    for s in range(steps):
        pos = pos_ref[s : s + 1, :]
        ids = lax.broadcasted_iota(jnp.int32, pos.shape, 1)
        spot = jnp.where(ids < count_ref[s], (pos % KW) * brows + pos // KW, KW * brows)
        row_ref[s : s + 1, 0:slots] = spot.astype(jnp.float32)
    out_ref[:, steps * flat :] = row_ref[...].astype(jnp.bfloat16)


def finish_kernel(parts_ref, out_ref, rows_ref):
    total = jnp.sum(parts_ref[...], axis=0)
    for j in range(total.shape[0] // TILES):
        for h in range(2):
            rows_ref[pl.ds(j * BLK + h, TILES, stride=2), :] = total[
                j * TILES : (j + 1) * TILES, h * LANES : (h + 1) * LANES
            ]
    out_ref[...] = rows_ref[...].astype(jnp.bfloat16)


def body(stiff_blocks, block_pos, block_count, modes, panel_owner):
    layers, nx, nz = lax.axis_size("layer"), lax.axis_size("x"), lax.axis_size("zb")
    x, core, zb, zc = (lax.axis_index(a) for a in ("x", "core", "zb", "zc"))
    slots = stiff_blocks.shape[4]
    brows = slots * 2 // KW
    width = modes.shape[3]
    depth = modes.shape[2]
    blks = depth // BLK

    def turn(v, k):
        pairs = [(c * nz + i, c * nz + (i + (k if c == 0 else -k)) % nz) for c in range(2) for i in range(nz)]
        return lax.ppermute(v, ("core", "zb"), pairs)

    own_piece = pl.pallas_call(
        functools.partial(pack_kernel, brows=brows),
        out_shape=jax.ShapeDtypeStruct((slots, STEPS * FLAT + LANES), jnp.bfloat16),
        scratch_shapes=[pltpu.VMEM((slots, LANES), jnp.float32)],
        in_specs=[pl.BlockSpec(memory_space=pltpu.VMEM)] * 2 + [pl.BlockSpec(memory_space=pltpu.SMEM)],
        name="pack",
    )(stiff_blocks[0, 0, 0], block_pos[0, 0, 0], block_count[0, 0, 0])

    half = nz // 2
    fwd, back = [own_piece], [own_piece]

    def after(value, *others):
        return lax.optimization_barrier((value, *others))

    mine = modes.reshape(STEPS * depth, width)
    far = lax.ppermute(mine, "zc", [(0, 1), (1, 0)])
    fwd.append(turn(fwd[0], 1))
    back[0], far = after(back[0], far)
    mine = jnp.concatenate([mine, far], axis=0)
    moved = [lax.ppermute(mine, "x", [(i, (i - k) % nx) for i in range(nx)]) for k in range(1, nx)]
    back.append(turn(back[0], -1))
    fwd.append(turn(fwd[1], 1))
    back[1], fwd[1] = after(back[1], fwd[1])
    back.append(turn(back[1], -1))
    fwd[2], back[1], *moved = after(fwd[2], back[1], *moved)
    fwd.append(turn(fwd[2], 1))
    back[2], fwd[2] = after(back[2], fwd[2])
    back.append(turn(back[2], -1))
    mine = jnp.concatenate([mine] + moved, axis=0)
    other = lax.ppermute(mine, "core", [(0, 1), (1, 0)])
    fwd[3], back[2], other = after(fwd[3], back[2], other)
    b = [v.reshape(-1, BLK, width) for v in (mine, other)]
    far_end = turn(fwd[3], 1)

    def number(away):
        sign = 1 - 2 * core
        return ((zb - sign * away) % nz) * GROUP + zc

    whole = lambda i: ((i, 0), (i, FLAT), (i, 2 * FLAT))
    own = panel_owner[0]
    call = functools.partial(product, brows=brows, slots=slots, blks=blks, layers=layers)

    def nums(aways):
        return jnp.stack([number(a) for a in aways] + [x, core, zc]).astype(jnp.int32)

    pieces, aways = [own_piece], [0]
    for i in range(1, half - 1):
        pieces += [fwd[i], back[i]]
        aways += [i, -i]
    acc = call(own, nums(aways), pieces, [whole(i) for i in range(len(pieces))], b, None, last=False)
    i = half - 1
    out = call(own, nums([i, -i, half]), [fwd[i], back[i], far_end], [whole(k) for k in range(3)], b, acc, last=True)
    out = lax.all_to_all(out, ("layer", "zc"), 0, 0, tiled=True)
    return pl.pallas_call(
        finish_kernel,
        out_shape=jax.ShapeDtypeStruct((brows * BLK // layers, width), jnp.bfloat16),
        scratch_shapes=[pltpu.VMEM((brows * BLK // layers, width), jnp.float32)],
        name="finish",
    )(out)


def solution(mesh):
    layers, rows, cols = (mesh.shape[a] for a in ("layer", "row", "col"))
    fine = Mesh(
        mesh.devices.reshape(layers, rows // 2, 2, cols // GROUP, GROUP), ("layer", "x", "core", "zb", "zc")
    )
    row, col = ("x", "core"), ("zb", "zc")
    return jax.shard_map(
        body,
        mesh=fine,
        in_specs=(
            P("layer", row, col, None, None, None),
            P("layer", row, col, None, None),
            P("layer", row, col, None),
            P("layer", None, row, col),
            P("layer", None, None),
        ),
        out_specs=P(row + ("layer",), col),
        check_vma=False,
    )
```

```python
import functools

import jax
import jax.numpy as jnp
from jax import lax
from jax.experimental import pallas as pl
from jax.experimental.pallas import tpu as pltpu
from jax.sharding import Mesh, PartitionSpec as P

BLK = 64
KW = 4
STEPS = 2
LANES = 128
TILES = BLK * BLK // LANES
FLAT = BLK * BLK
GROUP = 2


def product_kernel(*refs, parts, brows, slots, blks, group, first, last):
    own_ref, num_ref = refs[0], refs[1]
    count = max(ref for part in parts for ref, _ in part) + 1
    piece_refs = refs[2 : 2 + count]
    rest = refs[2 + count :]
    b_refs, rest = rest[:2], rest[2:]
    if not first:
        acc_in, rest = rest[0], rest[1:]
    out_ref, stage_ref, hot_ref, lhs_ref, rhs_ref, b_ref, sem = rest[:7]
    acc_ref = rest[7] if last else out_ref
    n = len(parts)
    width = KW * LANES
    chunk = group * LANES
    per_b = b_ref.shape[0] // 2

    copies = [
        pltpu.make_async_copy(b_refs[e], b_ref.at[pl.ds(e * per_b, per_b)], sem.at[e]) for e in range(2)
    ]
    for copy in copies:
        copy.start()
    for i, part in enumerate(parts):
        for s in range(STEPS):
            ref, off = part[s]
            stage_ref[i, s] = piece_refs[ref][:, off : off + FLAT]
            ref, off = part[STEPS]
            spot = piece_refs[ref][:, off : off + LANES].astype(jnp.float32)[s : s + 1, :slots]
            ids = lax.broadcasted_iota(jnp.int32, (KW * brows, slots), 0).astype(jnp.float32)
            hot_ref[i, s] = jnp.where(ids == spot, 1.0, 0.0).astype(jnp.bfloat16)
    rhs_ref[...] = jnp.zeros_like(rhs_ref)
    if first:
        acc_ref[...] = jnp.zeros_like(acc_ref)
    else:
        acc_ref[...] = acc_in[...]
    x, core = num_ref[n], num_ref[n + 1]
    for copy in copies:
        copy.wait()

    def one(i, carry):
        g0 = num_ref[i] * KW
        for s in range(STEPS):
            dense = jnp.dot(hot_ref[i, s], stage_ref[i, s], preferred_element_type=jnp.float32)
            for bc in range(KW):
                cols = jnp.concatenate(
                    [
                        dense[bc * brows : (bc + 1) * brows, k * LANES : (k + 1) * LANES]
                        for k in range(TILES)
                    ],
                    axis=0,
                )
                lhs_ref[:, s * width + bc * LANES : s * width + (bc + 1) * LANES] = cols.astype(jnp.bfloat16)
                p = own_ref[s, g0 + bc]
                row = p // blks
                side = (row % 2 + core) % 2
                ahead = (row // 2 + 4 - x) % 4
                for j in range(group):
                    at = (((side * 4 + ahead) * group + j) * STEPS + s) * blks + p % blks
                    blk = b_ref[at]
                    for h in range(2):
                        r = s * width + bc * LANES + h * BLK
                        c = h * chunk + j * LANES
                        rhs_ref[r : r + BLK, c : c + LANES] = blk
        more = jnp.dot(lhs_ref[...], rhs_ref[...], preferred_element_type=jnp.float32)
        for q in range(2 * group):
            acc_ref[q] += more[:, q * LANES : (q + 1) * LANES]
        return carry

    lax.fori_loop(0, n, one, 0)

    if last:
        zc = num_ref[n + 2]
        per_layer = out_ref.shape[1] // TILES
        layers = brows // per_layer
        for l in range(layers):
            for j in range(group):
                to = l * group + (zc + j) % group
                for m in range(per_layer):
                    for h in range(2):
                        out_ref[to, m * TILES : (m + 1) * TILES, h * LANES : (h + 1) * LANES] = acc_ref[
                            h * group + j, pl.ds(l * per_layer + m, TILES, stride=brows), :
                        ]


def product(own, nums, pieces, parts, b, acc, *, brows, slots, blks, layers, last):
    group = GROUP
    n = len(parts)
    first = acc is None
    rows = brows * TILES
    sums = jax.ShapeDtypeStruct((2 * group, rows, LANES), jnp.float32)
    outs = jax.ShapeDtypeStruct((layers * group, rows // layers, 2 * LANES), jnp.float32)
    vmem = pl.BlockSpec(memory_space=pltpu.VMEM)
    smem = pl.BlockSpec(memory_space=pltpu.SMEM)
    scratch = [
        pltpu.VMEM((n, STEPS, slots, FLAT), jnp.bfloat16),
        pltpu.VMEM((n, STEPS, KW * brows, slots), jnp.bfloat16),
        pltpu.VMEM((rows, STEPS * KW * LANES), jnp.bfloat16),
        pltpu.VMEM((STEPS * KW * LANES, 2 * group * LANES), jnp.bfloat16),
        pltpu.VMEM((2 * b[0].shape[0], BLK, LANES), jnp.bfloat16),
        pltpu.SemaphoreType.DMA((2,)),
    ]
    if last:
        scratch.append(pltpu.VMEM(sums.shape, jnp.float32))
    macs = n * STEPS * KW * LANES * rows * 2 * group * LANES
    return pl.pallas_call(
        functools.partial(
            product_kernel, parts=parts, brows=brows, slots=slots, blks=blks, group=group, first=first, last=last
        ),
        in_specs=[smem, smem] + [vmem] * len(pieces) + [pl.BlockSpec(memory_space=pl.ANY)] * 2 + [vmem] * (not first),
        out_specs=vmem,
        scratch_shapes=scratch,
        out_shape=outs if last else sums,
        compiler_params=pltpu.CompilerParams(vmem_limit_bytes=48 * 1024 * 1024),
        cost_estimate=pl.CostEstimate(flops=2 * macs, bytes_accessed=8 << 20, transcendentals=0),
        name="product_last" if last else "product",
    )(own, nums, *pieces, *b, *([] if first else [acc]))


def pack_kernel(stiff_ref, pos_ref, count_ref, out_ref, row_ref, *, brows):
    steps, slots, flat = stiff_ref.shape
    for s in range(steps):
        out_ref[:, s * flat : (s + 1) * flat] = stiff_ref[s]
    row_ref[...] = jnp.zeros_like(row_ref)
    for s in range(steps):
        pos = pos_ref[s : s + 1, :]
        ids = lax.broadcasted_iota(jnp.int32, pos.shape, 1)
        spot = jnp.where(ids < count_ref[s], (pos % KW) * brows + pos // KW, KW * brows)
        row_ref[s : s + 1, 0:slots] = spot.astype(jnp.float32)
    out_ref[:, steps * flat :] = row_ref[...].astype(jnp.bfloat16)


def finish_kernel(parts_ref, out_ref, rows_ref):
    total = jnp.sum(parts_ref[...], axis=0)
    for j in range(total.shape[0] // TILES):
        for h in range(2):
            rows_ref[pl.ds(j * BLK + h, TILES, stride=2), :] = total[
                j * TILES : (j + 1) * TILES, h * LANES : (h + 1) * LANES
            ]
    out_ref[...] = rows_ref[...].astype(jnp.bfloat16)


def body(stiff_blocks, block_pos, block_count, modes, panel_owner):
    layers, nx, nz = lax.axis_size("layer"), lax.axis_size("x"), lax.axis_size("zb")
    x, core, zb, zc = (lax.axis_index(a) for a in ("x", "core", "zb", "zc"))
    slots = stiff_blocks.shape[4]
    brows = slots * 2 // KW
    width = modes.shape[3]
    depth = modes.shape[2]
    blks = depth // BLK

    def turn(v, k):
        pairs = [(c * nz + i, c * nz + (i + (k if c == 0 else -k)) % nz) for c in range(2) for i in range(nz)]
        return lax.ppermute(v, ("core", "zb"), pairs)

    own_piece = pl.pallas_call(
        functools.partial(pack_kernel, brows=brows),
        out_shape=jax.ShapeDtypeStruct((slots, STEPS * FLAT + LANES), jnp.bfloat16),
        scratch_shapes=[pltpu.VMEM((slots, LANES), jnp.float32)],
        in_specs=[pl.BlockSpec(memory_space=pltpu.VMEM)] * 2 + [pl.BlockSpec(memory_space=pltpu.SMEM)],
        name="pack",
    )(stiff_blocks[0, 0, 0], block_pos[0, 0, 0], block_count[0, 0, 0])

    half = nz // 2
    fwd, back = [own_piece], [own_piece]

    def after(value, *others):
        return lax.optimization_barrier((value, *others))

    mine = modes.reshape(STEPS * depth, width)
    far = lax.ppermute(mine, "zc", [(0, 1), (1, 0)])
    fwd.append(turn(fwd[0], 1))
    back.append(turn(back[0], -1))
    fwd[1], far = after(fwd[1], far)
    fwd.append(turn(fwd[1], 1))
    mine = jnp.concatenate([mine, far], axis=0)
    moved = [lax.ppermute(mine, "x", [(i, (i - k) % nx) for i in range(nx)]) for k in range(1, nx)]
    back[1], fwd[1] = after(back[1], fwd[1])
    back.append(turn(back[1], -1))
    fwd[2], back[1] = after(fwd[2], back[1])
    fwd.append(turn(fwd[2], 1))
    back[2], fwd[2], *moved = after(back[2], fwd[2], *moved)
    back.append(turn(back[2], -1))
    mine = jnp.concatenate([mine] + moved, axis=0)
    other = lax.ppermute(mine, "core", [(0, 1), (1, 0)])
    fwd[3], back[2], other = after(fwd[3], back[2], other)
    b = [v.reshape(-1, BLK, width) for v in (mine, other)]
    far_end = turn(fwd[3], 1)

    def number(away):
        sign = 1 - 2 * core
        return ((zb - sign * away) % nz) * GROUP + zc

    whole = lambda i: ((i, 0), (i, FLAT), (i, 2 * FLAT))
    own = panel_owner[0]
    call = functools.partial(product, brows=brows, slots=slots, blks=blks, layers=layers)

    def nums(aways):
        return jnp.stack([number(a) for a in aways] + [x, core, zc]).astype(jnp.int32)

    pieces, aways = [own_piece], [0]
    for i in range(1, half - 1):
        pieces += [fwd[i], back[i]]
        aways += [i, -i]
    acc = call(own, nums(aways), pieces, [whole(i) for i in range(len(pieces))], b, None, last=False)
    i = half - 1
    out = call(own, nums([i, -i, half]), [fwd[i], back[i], far_end], [whole(k) for k in range(3)], b, acc, last=True)
    out = lax.all_to_all(out, ("layer", "zc"), 0, 0, tiled=True)
    return pl.pallas_call(
        finish_kernel,
        out_shape=jax.ShapeDtypeStruct((brows * BLK // layers, width), jnp.bfloat16),
        scratch_shapes=[pltpu.VMEM((brows * BLK // layers, width), jnp.float32)],
        name="finish",
    )(out)


def solution(mesh):
    layers, rows, cols = (mesh.shape[a] for a in ("layer", "row", "col"))
    fine = Mesh(
        mesh.devices.reshape(layers, rows // 2, 2, cols // GROUP, GROUP), ("layer", "x", "core", "zb", "zc")
    )
    row, col = ("x", "core"), ("zb", "zc")
    return jax.shard_map(
        body,
        mesh=fine,
        in_specs=(
            P("layer", row, col, None, None, None),
            P("layer", row, col, None, None),
            P("layer", row, col, None),
            P("layer", None, row, col),
            P("layer", None, None),
        ),
        out_specs=P(row + ("layer",), col),
        check_vma=False,
    )
```

```python
import functools

import jax
import jax.numpy as jnp
from jax import lax
from jax.experimental import pallas as pl
from jax.experimental.pallas import tpu as pltpu
from jax.sharding import Mesh, PartitionSpec as P

BLK = 64
KW = 4
STEPS = 2
LANES = 128
TILES = BLK * BLK // LANES
FLAT = BLK * BLK
GROUP = 2


def product_kernel(*refs, parts, brows, slots, blks, group, first, last):
    own_ref, num_ref = refs[0], refs[1]
    count = max(ref for part in parts for ref, _ in part) + 1
    piece_refs = refs[2 : 2 + count]
    rest = refs[2 + count :]
    b_refs, rest = rest[:2], rest[2:]
    if not first:
        acc_in, rest = rest[0], rest[1:]
    out_ref, stage_ref, hot_ref, lhs_ref, rhs_ref = rest[:5]
    acc_ref = rest[5] if last else out_ref
    n = len(parts)
    width = KW * LANES
    chunk = group * LANES

    for i, part in enumerate(parts):
        for s in range(STEPS):
            ref, off = part[s]
            stage_ref[i, s] = piece_refs[ref][:, off : off + FLAT]
            ref, off = part[STEPS]
            spot = piece_refs[ref][:, off : off + LANES].astype(jnp.float32)[s : s + 1, :slots]
            ids = lax.broadcasted_iota(jnp.int32, (KW * brows, slots), 0).astype(jnp.float32)
            hot_ref[i, s] = jnp.where(ids == spot, 1.0, 0.0).astype(jnp.bfloat16)
    rhs_ref[...] = jnp.zeros_like(rhs_ref)
    if first:
        acc_ref[...] = jnp.zeros_like(acc_ref)
    else:
        acc_ref[...] = acc_in[...]
    x, core = num_ref[n], num_ref[n + 1]

    def one(i, carry):
        g0 = num_ref[i] * KW
        for s in range(STEPS):
            dense = jnp.dot(hot_ref[i, s], stage_ref[i, s], preferred_element_type=jnp.float32)
            for bc in range(KW):
                cols = jnp.concatenate(
                    [
                        dense[bc * brows : (bc + 1) * brows, k * LANES : (k + 1) * LANES]
                        for k in range(TILES)
                    ],
                    axis=0,
                )
                lhs_ref[:, s * width + bc * LANES : s * width + (bc + 1) * LANES] = cols.astype(jnp.bfloat16)
                p = own_ref[s, g0 + bc]
                row = p // blks
                side = (row % 2 + core) % 2
                ahead = (row // 2 + 4 - x) % 4
                for j in range(group):
                    at = ((ahead * group + j) * STEPS + s) * blks + p % blks
                    blk = jnp.where(side == 0, b_refs[0][at], b_refs[1][at])
                    for h in range(2):
                        r = s * width + bc * LANES + h * BLK
                        c = h * chunk + j * LANES
                        rhs_ref[r : r + BLK, c : c + LANES] = blk
        more = jnp.dot(lhs_ref[...], rhs_ref[...], preferred_element_type=jnp.float32)
        for q in range(2 * group):
            acc_ref[q] += more[:, q * LANES : (q + 1) * LANES]
        return carry

    lax.fori_loop(0, n, one, 0)

    if last:
        zc = num_ref[n + 2]
        per_layer = out_ref.shape[1] // TILES
        layers = brows // per_layer
        for l in range(layers):
            for j in range(group):
                to = l * group + (zc + j) % group
                for m in range(per_layer):
                    for h in range(2):
                        out_ref[to, m * TILES : (m + 1) * TILES, h * LANES : (h + 1) * LANES] = acc_ref[
                            h * group + j, pl.ds(l * per_layer + m, TILES, stride=brows), :
                        ]


def product(own, nums, pieces, parts, b, acc, *, brows, slots, blks, layers, last):
    group = GROUP
    n = len(parts)
    first = acc is None
    rows = brows * TILES
    sums = jax.ShapeDtypeStruct((2 * group, rows, LANES), jnp.float32)
    outs = jax.ShapeDtypeStruct((layers * group, rows // layers, 2 * LANES), jnp.float32)
    vmem = pl.BlockSpec(memory_space=pltpu.VMEM)
    smem = pl.BlockSpec(memory_space=pltpu.SMEM)
    scratch = [
        pltpu.VMEM((n, STEPS, slots, FLAT), jnp.bfloat16),
        pltpu.VMEM((n, STEPS, KW * brows, slots), jnp.bfloat16),
        pltpu.VMEM((rows, STEPS * KW * LANES), jnp.bfloat16),
        pltpu.VMEM((STEPS * KW * LANES, 2 * group * LANES), jnp.bfloat16),
    ]
    if last:
        scratch.append(pltpu.VMEM(sums.shape, jnp.float32))
    macs = n * STEPS * KW * LANES * rows * 2 * group * LANES
    return pl.pallas_call(
        functools.partial(
            product_kernel, parts=parts, brows=brows, slots=slots, blks=blks, group=group, first=first, last=last
        ),
        in_specs=[smem, smem] + [vmem] * (len(pieces) + 2 + (not first)),
        out_specs=vmem,
        scratch_shapes=scratch,
        out_shape=outs if last else sums,
        compiler_params=pltpu.CompilerParams(vmem_limit_bytes=20 * 1024 * 1024),
        cost_estimate=pl.CostEstimate(flops=2 * macs, bytes_accessed=8 << 20, transcendentals=0),
        name="product_last" if last else "product",
    )(own, nums, *pieces, *b, *([] if first else [acc]))


def pack_kernel(stiff_ref, pos_ref, count_ref, out_ref, row_ref, *, brows):
    steps, slots, flat = stiff_ref.shape
    for s in range(steps):
        out_ref[:, s * flat : (s + 1) * flat] = stiff_ref[s]
    row_ref[...] = jnp.zeros_like(row_ref)
    for s in range(steps):
        pos = pos_ref[s : s + 1, :]
        ids = lax.broadcasted_iota(jnp.int32, pos.shape, 1)
        spot = jnp.where(ids < count_ref[s], (pos % KW) * brows + pos // KW, KW * brows)
        row_ref[s : s + 1, 0:slots] = spot.astype(jnp.float32)
    out_ref[:, steps * flat :] = row_ref[...].astype(jnp.bfloat16)


def finish_kernel(parts_ref, out_ref, rows_ref):
    total = jnp.sum(parts_ref[...], axis=0)
    for j in range(total.shape[0] // TILES):
        for h in range(2):
            rows_ref[pl.ds(j * BLK + h, TILES, stride=2), :] = total[
                j * TILES : (j + 1) * TILES, h * LANES : (h + 1) * LANES
            ]
    out_ref[...] = rows_ref[...].astype(jnp.bfloat16)


def body(stiff_blocks, block_pos, block_count, modes, panel_owner):
    layers, nx, nz = lax.axis_size("layer"), lax.axis_size("x"), lax.axis_size("zb")
    x, core, zb, zc = (lax.axis_index(a) for a in ("x", "core", "zb", "zc"))
    slots = stiff_blocks.shape[4]
    brows = slots * 2 // KW
    width = modes.shape[3]
    depth = modes.shape[2]
    blks = depth // BLK

    def turn(v, k):
        pairs = [(c * nz + i, c * nz + (i + (k if c == 0 else -k)) % nz) for c in range(2) for i in range(nz)]
        return lax.ppermute(v, ("core", "zb"), pairs)

    own_piece = pl.pallas_call(
        functools.partial(pack_kernel, brows=brows),
        out_shape=jax.ShapeDtypeStruct((slots, STEPS * FLAT + LANES), jnp.bfloat16),
        scratch_shapes=[pltpu.VMEM((slots, LANES), jnp.float32)],
        in_specs=[pl.BlockSpec(memory_space=pltpu.VMEM)] * 2 + [pl.BlockSpec(memory_space=pltpu.SMEM)],
        name="pack",
    )(stiff_blocks[0, 0, 0], block_pos[0, 0, 0], block_count[0, 0, 0])

    half = nz // 2
    fwd, back = [own_piece], [own_piece]

    def after(value, *others):
        return lax.optimization_barrier((value, *others))

    mine = modes.reshape(STEPS * depth, width)
    far = lax.ppermute(mine, "zc", [(0, 1), (1, 0)])
    fwd.append(turn(fwd[0], 1))
    back[0], far = after(back[0], far)
    mine = jnp.concatenate([mine, far], axis=0)
    moved = [lax.ppermute(mine, "x", [(i, (i - k) % nx) for i in range(nx)]) for k in range(1, nx)]
    back.append(turn(back[0], -1))
    fwd.append(turn(fwd[1], 1))
    back[1], fwd[1] = after(back[1], fwd[1])
    back.append(turn(back[1], -1))
    fwd[2], back[1], *moved = after(fwd[2], back[1], *moved)
    fwd.append(turn(fwd[2], 1))
    back[2], fwd[2] = after(back[2], fwd[2])
    back.append(turn(back[2], -1))
    mine = jnp.concatenate([mine] + moved, axis=0)
    other = lax.ppermute(mine, "core", [(0, 1), (1, 0)])
    fwd[3], back[2], other = after(fwd[3], back[2], other)
    b = [v.reshape(-1, BLK, width) for v in (mine, other)]
    far_end = turn(fwd[3], 1)

    def number(away):
        sign = 1 - 2 * core
        return ((zb - sign * away) % nz) * GROUP + zc

    whole = lambda i: ((i, 0), (i, FLAT), (i, 2 * FLAT))
    own = panel_owner[0]
    call = functools.partial(product, brows=brows, slots=slots, blks=blks, layers=layers)

    def nums(aways):
        return jnp.stack([number(a) for a in aways] + [x, core, zc]).astype(jnp.int32)

    pieces, aways = [own_piece], [0]
    for i in range(1, half - 1):
        pieces += [fwd[i], back[i]]
        aways += [i, -i]
    acc = call(own, nums(aways), pieces, [whole(i) for i in range(len(pieces))], b, None, last=False)
    i = half - 1
    out = call(own, nums([i, -i, half]), [fwd[i], back[i], far_end], [whole(k) for k in range(3)], b, acc, last=True)
    out = lax.all_to_all(out, ("layer", "zc"), 0, 0, tiled=True)
    return pl.pallas_call(
        finish_kernel,
        out_shape=jax.ShapeDtypeStruct((brows * BLK // layers, width), jnp.bfloat16),
        scratch_shapes=[pltpu.VMEM((brows * BLK // layers, width), jnp.float32)],
        name="finish",
    )(out)


def solution(mesh):
    layers, rows, cols = (mesh.shape[a] for a in ("layer", "row", "col"))
    fine = Mesh(
        mesh.devices.reshape(layers, rows // 2, 2, cols // GROUP, GROUP), ("layer", "x", "core", "zb", "zc")
    )
    row, col = ("x", "core"), ("zb", "zc")
    return jax.shard_map(
        body,
        mesh=fine,
        in_specs=(
            P("layer", row, col, None, None, None),
            P("layer", row, col, None, None),
            P("layer", row, col, None),
            P("layer", None, row, col),
            P("layer", None, None),
        ),
        out_specs=P(row + ("layer",), col),
        check_vma=False,
    )
```

```python
import functools

import jax
import jax.numpy as jnp
from jax import lax
from jax.experimental import pallas as pl
from jax.experimental.pallas import tpu as pltpu
from jax.sharding import Mesh, PartitionSpec as P

BLK = 64
KW = 4
STEPS = 2
LANES = 128
TILES = BLK * BLK // LANES
FLAT = BLK * BLK
GROUP = 2


def product_kernel(*refs, parts, brows, slots, blks, group, first, last):
    own_ref, num_ref = refs[0], refs[1]
    count = max(ref for part in parts for ref, _ in part) + 1
    piece_refs = refs[2 : 2 + count]
    rest = refs[2 + count :]
    b_refs, rest = rest[:2], rest[2:]
    if not first:
        acc_in, rest = rest[0], rest[1:]
    out_ref, stage_ref, hot_ref, lhs_ref, rhs_ref = rest[:5]
    acc_ref = rest[5] if last else out_ref
    n = len(parts)
    width = KW * LANES
    chunk = group * LANES

    for i, part in enumerate(parts):
        for s in range(STEPS):
            ref, off = part[s]
            stage_ref[i, s] = piece_refs[ref][:, off : off + FLAT]
            ref, off = part[STEPS]
            spot = piece_refs[ref][:, off : off + LANES].astype(jnp.float32)[s : s + 1, :slots]
            ids = lax.broadcasted_iota(jnp.int32, (KW * brows, slots), 0).astype(jnp.float32)
            hot_ref[i, s] = jnp.where(ids == spot, 1.0, 0.0).astype(jnp.bfloat16)
    rhs_ref[...] = jnp.zeros_like(rhs_ref)
    if first:
        acc_ref[...] = jnp.zeros_like(acc_ref)
    else:
        acc_ref[...] = acc_in[...]
    x, core = num_ref[n], num_ref[n + 1]

    def one(i, carry):
        g0 = num_ref[i] * KW
        for s in range(STEPS):
            dense = jnp.dot(hot_ref[i, s], stage_ref[i, s], preferred_element_type=jnp.float32)
            for bc in range(KW):
                cols = jnp.concatenate(
                    [
                        dense[bc * brows : (bc + 1) * brows, k * LANES : (k + 1) * LANES]
                        for k in range(TILES)
                    ],
                    axis=0,
                )
                lhs_ref[:, s * width + bc * LANES : s * width + (bc + 1) * LANES] = cols.astype(jnp.bfloat16)
                p = own_ref[s, g0 + bc]
                row = p // blks
                side = (row % 2 + core) % 2
                ahead = (row // 2 + 4 - x) % 4
                for j in range(group):
                    at = ((ahead * group + j) * STEPS + s) * blks + p % blks
                    blk = jnp.where(side == 0, b_refs[0][at], b_refs[1][at])
                    for h in range(2):
                        r = s * width + bc * LANES + h * BLK
                        c = h * chunk + j * LANES
                        rhs_ref[r : r + BLK, c : c + LANES] = blk
        more = jnp.dot(lhs_ref[...], rhs_ref[...], preferred_element_type=jnp.float32)
        for q in range(2 * group):
            acc_ref[q] += more[:, q * LANES : (q + 1) * LANES]
        return carry

    lax.fori_loop(0, n, one, 0)

    if last:
        zc = num_ref[n + 2]
        per_layer = out_ref.shape[1] // TILES
        layers = brows // per_layer
        for l in range(layers):
            for j in range(group):
                to = l * group + (zc + j) % group
                for m in range(per_layer):
                    for h in range(2):
                        out_ref[to, m * TILES : (m + 1) * TILES, h * LANES : (h + 1) * LANES] = acc_ref[
                            h * group + j, pl.ds(l * per_layer + m, TILES, stride=brows), :
                        ]


def product(own, nums, pieces, parts, b, acc, *, brows, slots, blks, layers, last):
    group = GROUP
    n = len(parts)
    first = acc is None
    rows = brows * TILES
    sums = jax.ShapeDtypeStruct((2 * group, rows, LANES), jnp.float32)
    outs = jax.ShapeDtypeStruct((layers * group, rows // layers, 2 * LANES), jnp.float32)
    vmem = pl.BlockSpec(memory_space=pltpu.VMEM)
    smem = pl.BlockSpec(memory_space=pltpu.SMEM)
    scratch = [
        pltpu.VMEM((n, STEPS, slots, FLAT), jnp.bfloat16),
        pltpu.VMEM((n, STEPS, KW * brows, slots), jnp.bfloat16),
        pltpu.VMEM((rows, STEPS * KW * LANES), jnp.bfloat16),
        pltpu.VMEM((STEPS * KW * LANES, 2 * group * LANES), jnp.bfloat16),
    ]
    if last:
        scratch.append(pltpu.VMEM(sums.shape, jnp.float32))
    macs = n * STEPS * KW * LANES * rows * 2 * group * LANES
    return pl.pallas_call(
        functools.partial(
            product_kernel, parts=parts, brows=brows, slots=slots, blks=blks, group=group, first=first, last=last
        ),
        in_specs=[smem, smem] + [vmem] * (len(pieces) + 2 + (not first)),
        out_specs=vmem,
        scratch_shapes=scratch,
        out_shape=outs if last else sums,
        compiler_params=pltpu.CompilerParams(vmem_limit_bytes=20 * 1024 * 1024),
        cost_estimate=pl.CostEstimate(flops=2 * macs, bytes_accessed=8 << 20, transcendentals=0),
        name="product_last" if last else "product",
    )(own, nums, *pieces, *b, *([] if first else [acc]))


def pack_kernel(stiff_ref, pos_ref, count_ref, out_ref, row_ref, *, brows):
    steps, slots, flat = stiff_ref.shape
    for s in range(steps):
        out_ref[:, s * flat : (s + 1) * flat] = stiff_ref[s]
    row_ref[...] = jnp.zeros_like(row_ref)
    for s in range(steps):
        pos = pos_ref[s : s + 1, :]
        ids = lax.broadcasted_iota(jnp.int32, pos.shape, 1)
        spot = jnp.where(ids < count_ref[s], (pos % KW) * brows + pos // KW, KW * brows)
        row_ref[s : s + 1, 0:slots] = spot.astype(jnp.float32)
    out_ref[:, steps * flat :] = row_ref[...].astype(jnp.bfloat16)


def finish_kernel(parts_ref, out_ref, rows_ref):
    total = jnp.sum(parts_ref[...], axis=0)
    for j in range(total.shape[0] // TILES):
        for h in range(2):
            rows_ref[pl.ds(j * BLK + h, TILES, stride=2), :] = total[
                j * TILES : (j + 1) * TILES, h * LANES : (h + 1) * LANES
            ]
    out_ref[...] = rows_ref[...].astype(jnp.bfloat16)


def body(stiff_blocks, block_pos, block_count, modes, panel_owner):
    layers, nx, nz = lax.axis_size("layer"), lax.axis_size("x"), lax.axis_size("zb")
    x, core, zb, zc = (lax.axis_index(a) for a in ("x", "core", "zb", "zc"))
    slots = stiff_blocks.shape[4]
    brows = slots * 2 // KW
    width = modes.shape[3]
    depth = modes.shape[2]
    blks = depth // BLK

    def turn(v, k):
        pairs = [(c * nz + i, c * nz + (i + (k if c == 0 else -k)) % nz) for c in range(2) for i in range(nz)]
        return lax.ppermute(v, ("core", "zb"), pairs)

    own_piece = pl.pallas_call(
        functools.partial(pack_kernel, brows=brows),
        out_shape=jax.ShapeDtypeStruct((slots, STEPS * FLAT + LANES), jnp.bfloat16),
        scratch_shapes=[pltpu.VMEM((slots, LANES), jnp.float32)],
        in_specs=[pl.BlockSpec(memory_space=pltpu.VMEM)] * 2 + [pl.BlockSpec(memory_space=pltpu.SMEM)],
        name="pack",
    )(stiff_blocks[0, 0, 0], block_pos[0, 0, 0], block_count[0, 0, 0])

    half = nz // 2
    fwd, back = [own_piece], [own_piece]

    def after(value, *others):
        return lax.optimization_barrier((value, *others))

    mine = modes.reshape(STEPS * depth, width)
    far = lax.ppermute(mine, "zc", [(0, 1), (1, 0)])
    fwd.append(turn(fwd[0], 1))
    back[0], far = after(back[0], far)
    mine = jnp.concatenate([mine, far], axis=0)
    moved = [lax.ppermute(mine, "x", [(i, (i - k) % nx) for i in range(nx)]) for k in range(1, nx)]
    back.append(turn(back[0], -1))
    fwd.append(turn(fwd[1], 1))
    back.append(turn(back[0], -2))
    fwd[2], back[1], *moved = after(fwd[2], back[1], *moved)
    fwd.append(turn(fwd[2], 1))
    back[2], fwd[2] = after(back[2], fwd[2])
    back.append(turn(back[2], -1))
    mine = jnp.concatenate([mine] + moved, axis=0)
    other = lax.ppermute(mine, "core", [(0, 1), (1, 0)])
    fwd[3], back[2], other = after(fwd[3], back[2], other)
    b = [v.reshape(-1, BLK, width) for v in (mine, other)]
    far_end = turn(fwd[3], 1)

    def number(away):
        sign = 1 - 2 * core
        return ((zb - sign * away) % nz) * GROUP + zc

    whole = lambda i: ((i, 0), (i, FLAT), (i, 2 * FLAT))
    own = panel_owner[0]
    call = functools.partial(product, brows=brows, slots=slots, blks=blks, layers=layers)

    def nums(aways):
        return jnp.stack([number(a) for a in aways] + [x, core, zc]).astype(jnp.int32)

    pieces, aways = [own_piece], [0]
    for i in range(1, half - 1):
        pieces += [fwd[i], back[i]]
        aways += [i, -i]
    acc = call(own, nums(aways), pieces, [whole(i) for i in range(len(pieces))], b, None, last=False)
    i = half - 1
    out = call(own, nums([i, -i, half]), [fwd[i], back[i], far_end], [whole(k) for k in range(3)], b, acc, last=True)
    out = lax.all_to_all(out, ("layer", "zc"), 0, 0, tiled=True)
    return pl.pallas_call(
        finish_kernel,
        out_shape=jax.ShapeDtypeStruct((brows * BLK // layers, width), jnp.bfloat16),
        scratch_shapes=[pltpu.VMEM((brows * BLK // layers, width), jnp.float32)],
        name="finish",
    )(out)


def solution(mesh):
    layers, rows, cols = (mesh.shape[a] for a in ("layer", "row", "col"))
    fine = Mesh(
        mesh.devices.reshape(layers, rows // 2, 2, cols // GROUP, GROUP), ("layer", "x", "core", "zb", "zc")
    )
    row, col = ("x", "core"), ("zb", "zc")
    return jax.shard_map(
        body,
        mesh=fine,
        in_specs=(
            P("layer", row, col, None, None, None),
            P("layer", row, col, None, None),
            P("layer", row, col, None),
            P("layer", None, row, col),
            P("layer", None, None),
        ),
        out_specs=P(row + ("layer",), col),
        check_vma=False,
    )
```

```python
import functools

import jax
import jax.numpy as jnp
from jax import lax
from jax.experimental import pallas as pl
from jax.experimental.pallas import tpu as pltpu
from jax.sharding import Mesh, PartitionSpec as P

BLK = 64
KW = 4
STEPS = 2
LANES = 128
TILES = BLK * BLK // LANES
FLAT = BLK * BLK
GROUP = 2


def product_kernel(*refs, parts, brows, slots, blks, group, first, last):
    own_ref, num_ref = refs[0], refs[1]
    count = max(ref for part in parts for ref, _ in part) + 1
    piece_refs = refs[2 : 2 + count]
    rest = refs[2 + count :]
    b_refs, rest = rest[:2], rest[2:]
    if not first:
        acc_in, rest = rest[0], rest[1:]
    out_ref, stage_ref, hot_ref, lhs_ref, rhs_ref, b_ref, sem = rest[:7]
    acc_ref = rest[7] if last else out_ref
    n = len(parts)
    width = KW * LANES
    chunk = group * LANES
    per_b = b_ref.shape[0] // 2

    copies = [
        pltpu.make_async_copy(b_refs[e], b_ref.at[pl.ds(e * per_b, per_b)], sem.at[e]) for e in range(2)
    ]
    for copy in copies:
        copy.start()
    for i, part in enumerate(parts):
        for s in range(STEPS):
            ref, off = part[s]
            stage_ref[i, s] = piece_refs[ref][:, off : off + FLAT]
            ref, off = part[STEPS]
            spot = piece_refs[ref][:, off : off + LANES].astype(jnp.float32)[s : s + 1, :slots]
            ids = lax.broadcasted_iota(jnp.int32, (KW * brows, slots), 0).astype(jnp.float32)
            hot_ref[i, s] = jnp.where(ids == spot, 1.0, 0.0).astype(jnp.bfloat16)
    rhs_ref[...] = jnp.zeros_like(rhs_ref)
    if first:
        acc_ref[...] = jnp.zeros_like(acc_ref)
    else:
        acc_ref[...] = acc_in[...]
    x, core = num_ref[n], num_ref[n + 1]
    for copy in copies:
        copy.wait()

    def one(i, carry):
        g0 = num_ref[i] * KW
        for s in range(STEPS):
            dense = jnp.dot(hot_ref[i, s], stage_ref[i, s], preferred_element_type=jnp.float32)
            for bc in range(KW):
                cols = jnp.concatenate(
                    [
                        dense[bc * brows : (bc + 1) * brows, k * LANES : (k + 1) * LANES]
                        for k in range(TILES)
                    ],
                    axis=0,
                )
                lhs_ref[:, s * width + bc * LANES : s * width + (bc + 1) * LANES] = cols.astype(jnp.bfloat16)
                p = own_ref[s, g0 + bc]
                row = p // blks
                side = (row % 2 + core) % 2
                ahead = (row // 2 + 4 - x) % 4
                for j in range(group):
                    at = (((side * 4 + ahead) * group + j) * STEPS + s) * blks + p % blks
                    blk = b_ref[at]
                    for h in range(2):
                        r = s * width + bc * LANES + h * BLK
                        c = h * chunk + j * LANES
                        rhs_ref[r : r + BLK, c : c + LANES] = blk
        more = jnp.dot(lhs_ref[...], rhs_ref[...], preferred_element_type=jnp.float32)
        for q in range(2 * group):
            acc_ref[q] += more[:, q * LANES : (q + 1) * LANES]
        return carry

    lax.fori_loop(0, n, one, 0)

    if last:
        zc = num_ref[n + 2]
        per_layer = out_ref.shape[1] // TILES
        layers = brows // per_layer
        for l in range(layers):
            for j in range(group):
                to = l * group + (zc + j) % group
                for m in range(per_layer):
                    for h in range(2):
                        out_ref[to, m * TILES : (m + 1) * TILES, h * LANES : (h + 1) * LANES] = acc_ref[
                            h * group + j, pl.ds(l * per_layer + m, TILES, stride=brows), :
                        ]


def product(own, nums, pieces, parts, b, acc, *, brows, slots, blks, layers, last):
    group = GROUP
    n = len(parts)
    first = acc is None
    rows = brows * TILES
    sums = jax.ShapeDtypeStruct((2 * group, rows, LANES), jnp.float32)
    outs = jax.ShapeDtypeStruct((layers * group, rows // layers, 2 * LANES), jnp.float32)
    vmem = pl.BlockSpec(memory_space=pltpu.VMEM)
    smem = pl.BlockSpec(memory_space=pltpu.SMEM)
    scratch = [
        pltpu.VMEM((n, STEPS, slots, FLAT), jnp.bfloat16),
        pltpu.VMEM((n, STEPS, KW * brows, slots), jnp.bfloat16),
        pltpu.VMEM((rows, STEPS * KW * LANES), jnp.bfloat16),
        pltpu.VMEM((STEPS * KW * LANES, 2 * group * LANES), jnp.bfloat16),
        pltpu.VMEM((2 * b[0].shape[0], BLK, LANES), jnp.bfloat16),
        pltpu.SemaphoreType.DMA((2,)),
    ]
    if last:
        scratch.append(pltpu.VMEM(sums.shape, jnp.float32))
    macs = n * STEPS * KW * LANES * rows * 2 * group * LANES
    return pl.pallas_call(
        functools.partial(
            product_kernel, parts=parts, brows=brows, slots=slots, blks=blks, group=group, first=first, last=last
        ),
        in_specs=[smem, smem] + [vmem] * len(pieces) + [pl.BlockSpec(memory_space=pltpu.HBM)] * 2 + [vmem] * (not first),
        out_specs=vmem,
        scratch_shapes=scratch,
        out_shape=outs if last else sums,
        compiler_params=pltpu.CompilerParams(vmem_limit_bytes=20 * 1024 * 1024),
        cost_estimate=pl.CostEstimate(flops=2 * macs, bytes_accessed=8 << 20, transcendentals=0),
        name="product_last" if last else "product",
    )(own, nums, *pieces, *b, *([] if first else [acc]))


def pack_kernel(stiff_ref, pos_ref, count_ref, out_ref, row_ref, *, brows):
    steps, slots, flat = stiff_ref.shape
    for s in range(steps):
        out_ref[:, s * flat : (s + 1) * flat] = stiff_ref[s]
    row_ref[...] = jnp.zeros_like(row_ref)
    for s in range(steps):
        pos = pos_ref[s : s + 1, :]
        ids = lax.broadcasted_iota(jnp.int32, pos.shape, 1)
        spot = jnp.where(ids < count_ref[s], (pos % KW) * brows + pos // KW, KW * brows)
        row_ref[s : s + 1, 0:slots] = spot.astype(jnp.float32)
    out_ref[:, steps * flat :] = row_ref[...].astype(jnp.bfloat16)


def finish_kernel(parts_ref, out_ref, rows_ref):
    total = jnp.sum(parts_ref[...], axis=0)
    for j in range(total.shape[0] // TILES):
        for h in range(2):
            rows_ref[pl.ds(j * BLK + h, TILES, stride=2), :] = total[
                j * TILES : (j + 1) * TILES, h * LANES : (h + 1) * LANES
            ]
    out_ref[...] = rows_ref[...].astype(jnp.bfloat16)


def body(stiff_blocks, block_pos, block_count, modes, panel_owner):
    layers, nx, nz = lax.axis_size("layer"), lax.axis_size("x"), lax.axis_size("zb")
    x, core, zb, zc = (lax.axis_index(a) for a in ("x", "core", "zb", "zc"))
    slots = stiff_blocks.shape[4]
    brows = slots * 2 // KW
    width = modes.shape[3]
    depth = modes.shape[2]
    blks = depth // BLK

    def turn(v, k):
        pairs = [(c * nz + i, c * nz + (i + (k if c == 0 else -k)) % nz) for c in range(2) for i in range(nz)]
        return lax.ppermute(v, ("core", "zb"), pairs)

    own_piece = pl.pallas_call(
        functools.partial(pack_kernel, brows=brows),
        out_shape=jax.ShapeDtypeStruct((slots, STEPS * FLAT + LANES), jnp.bfloat16),
        scratch_shapes=[pltpu.VMEM((slots, LANES), jnp.float32)],
        in_specs=[pl.BlockSpec(memory_space=pltpu.VMEM)] * 2 + [pl.BlockSpec(memory_space=pltpu.SMEM)],
        name="pack",
    )(stiff_blocks[0, 0, 0], block_pos[0, 0, 0], block_count[0, 0, 0])

    half = nz // 2
    fwd, back = [own_piece], [own_piece]

    def after(value, *others):
        return lax.optimization_barrier((value, *others))

    mine = modes.reshape(STEPS * depth, width)
    far = lax.ppermute(mine, "zc", [(0, 1), (1, 0)])
    fwd.append(turn(fwd[0], 1))
    back[0], far = after(back[0], far)
    mine = jnp.concatenate([mine, far], axis=0)
    moved = [lax.ppermute(mine, "x", [(i, (i - k) % nx) for i in range(nx)]) for k in range(1, nx)]
    back.append(turn(back[0], -1))
    fwd.append(turn(fwd[1], 1))
    back[1], fwd[1] = after(back[1], fwd[1])
    back.append(turn(back[1], -1))
    fwd[2], back[1], *moved = after(fwd[2], back[1], *moved)
    fwd.append(turn(fwd[2], 1))
    back[2], fwd[2] = after(back[2], fwd[2])
    back.append(turn(back[2], -1))
    mine = jnp.concatenate([mine] + moved, axis=0)
    other = lax.ppermute(mine, "core", [(0, 1), (1, 0)])
    fwd[3], back[2], other = after(fwd[3], back[2], other)
    b = [v.reshape(-1, BLK, width) for v in (mine, other)]
    far_end = turn(fwd[3], 1)

    def number(away):
        sign = 1 - 2 * core
        return ((zb - sign * away) % nz) * GROUP + zc

    whole = lambda i: ((i, 0), (i, FLAT), (i, 2 * FLAT))
    own = panel_owner[0]
    call = functools.partial(product, brows=brows, slots=slots, blks=blks, layers=layers)

    def nums(aways):
        return jnp.stack([number(a) for a in aways] + [x, core, zc]).astype(jnp.int32)

    pieces, aways = [own_piece], [0]
    for i in range(1, half - 1):
        pieces += [fwd[i], back[i]]
        aways += [i, -i]
    acc = call(own, nums(aways), pieces, [whole(i) for i in range(len(pieces))], b, None, last=False)
    i = half - 1
    out = call(own, nums([i, -i, half]), [fwd[i], back[i], far_end], [whole(k) for k in range(3)], b, acc, last=True)
    out = lax.all_to_all(out, ("layer", "zc"), 0, 0, tiled=True)
    return pl.pallas_call(
        finish_kernel,
        out_shape=jax.ShapeDtypeStruct((brows * BLK // layers, width), jnp.bfloat16),
        scratch_shapes=[pltpu.VMEM((brows * BLK // layers, width), jnp.float32)],
        name="finish",
    )(out)


def solution(mesh):
    layers, rows, cols = (mesh.shape[a] for a in ("layer", "row", "col"))
    fine = Mesh(
        mesh.devices.reshape(layers, rows // 2, 2, cols // GROUP, GROUP), ("layer", "x", "core", "zb", "zc")
    )
    row, col = ("x", "core"), ("zb", "zc")
    return jax.shard_map(
        body,
        mesh=fine,
        in_specs=(
            P("layer", row, col, None, None, None),
            P("layer", row, col, None, None),
            P("layer", row, col, None),
            P("layer", None, row, col),
            P("layer", None, None),
        ),
        out_specs=P(row + ("layer",), col),
        check_vma=False,
    )
```

```python
import functools

import jax
import jax.numpy as jnp
from jax import lax
from jax.experimental import pallas as pl
from jax.experimental.pallas import tpu as pltpu
from jax.sharding import Mesh, PartitionSpec as P

BLK = 64
KW = 4
STEPS = 2
LANES = 128
TILES = BLK * BLK // LANES
FLAT = BLK * BLK
GROUP = 2


def product_kernel(*refs, parts, brows, slots, blks, group, first, last):
    own_ref, num_ref = refs[0], refs[1]
    count = max(ref for part in parts for ref, _ in part) + 1
    piece_refs = refs[2 : 2 + count]
    rest = refs[2 + count :]
    b_refs, rest = rest[:2], rest[2:]
    if not first:
        acc_in, rest = rest[0], rest[1:]
    out_ref, stage_ref, hot_ref, lhs_ref, rhs_ref = rest[:5]
    acc_ref = rest[5] if last else out_ref
    n = len(parts)
    width = KW * LANES
    chunk = group * LANES

    for i, part in enumerate(parts):
        for s in range(STEPS):
            ref, off = part[s]
            stage_ref[i, s] = piece_refs[ref][:, off : off + FLAT]
            ref, off = part[STEPS]
            spot = piece_refs[ref][:, off : off + LANES].astype(jnp.float32)[s : s + 1, :slots]
            ids = lax.broadcasted_iota(jnp.int32, (KW * brows, slots), 0).astype(jnp.float32)
            hot_ref[i, s] = jnp.where(ids == spot, 1.0, 0.0).astype(jnp.bfloat16)
    rhs_ref[...] = jnp.zeros_like(rhs_ref)
    if first:
        acc_ref[...] = jnp.zeros_like(acc_ref)
    else:
        acc_ref[...] = acc_in[...]
    x, core = num_ref[n], num_ref[n + 1]

    def one(i, carry):
        g0 = num_ref[i] * KW
        for s in range(STEPS):
            dense = jnp.dot(hot_ref[i, s], stage_ref[i, s], preferred_element_type=jnp.float32)
            for bc in range(KW):
                cols = jnp.concatenate(
                    [
                        dense[bc * brows : (bc + 1) * brows, k * LANES : (k + 1) * LANES]
                        for k in range(TILES)
                    ],
                    axis=0,
                )
                lhs_ref[:, s * width + bc * LANES : s * width + (bc + 1) * LANES] = cols.astype(jnp.bfloat16)
                p = own_ref[s, g0 + bc]
                row = p // blks
                side = (row % 2 + core) % 2
                ahead = (row // 2 + 4 - x) % 4
                for j in range(group):
                    at = ((ahead * group + j) * STEPS + s) * blks + p % blks
                    blk = jnp.where(side == 0, b_refs[0][at], b_refs[1][at])
                    for h in range(2):
                        r = s * width + bc * LANES + h * BLK
                        c = h * chunk + j * LANES
                        rhs_ref[r : r + BLK, c : c + LANES] = blk
        more = jnp.dot(lhs_ref[...], rhs_ref[...], preferred_element_type=jnp.float32)
        for q in range(2 * group):
            acc_ref[q] += more[:, q * LANES : (q + 1) * LANES]
        return carry

    lax.fori_loop(0, n, one, 0)

    if last:
        zc = num_ref[n + 2]
        per_layer = out_ref.shape[1] // TILES
        layers = brows // per_layer
        for l in range(layers):
            for j in range(group):
                to = l * group + (zc + j) % group
                for m in range(per_layer):
                    for h in range(2):
                        out_ref[to, m * TILES : (m + 1) * TILES, h * LANES : (h + 1) * LANES] = acc_ref[
                            h * group + j, pl.ds(l * per_layer + m, TILES, stride=brows), :
                        ]


def product(own, nums, pieces, parts, b, acc, *, brows, slots, blks, layers, last):
    group = GROUP
    n = len(parts)
    first = acc is None
    rows = brows * TILES
    sums = jax.ShapeDtypeStruct((2 * group, rows, LANES), jnp.float32)
    outs = jax.ShapeDtypeStruct((layers * group, rows // layers, 2 * LANES), jnp.float32)
    vmem = pl.BlockSpec(memory_space=pltpu.VMEM)
    smem = pl.BlockSpec(memory_space=pltpu.SMEM)
    scratch = [
        pltpu.VMEM((n, STEPS, slots, FLAT), jnp.bfloat16),
        pltpu.VMEM((n, STEPS, KW * brows, slots), jnp.bfloat16),
        pltpu.VMEM((rows, STEPS * KW * LANES), jnp.bfloat16),
        pltpu.VMEM((STEPS * KW * LANES, 2 * group * LANES), jnp.bfloat16),
    ]
    if last:
        scratch.append(pltpu.VMEM(sums.shape, jnp.float32))
    macs = n * STEPS * KW * LANES * rows * 2 * group * LANES
    return pl.pallas_call(
        functools.partial(
            product_kernel, parts=parts, brows=brows, slots=slots, blks=blks, group=group, first=first, last=last
        ),
        in_specs=[smem, smem] + [vmem] * (len(pieces) + 2 + (not first)),
        out_specs=vmem,
        scratch_shapes=scratch,
        out_shape=outs if last else sums,
        compiler_params=pltpu.CompilerParams(vmem_limit_bytes=20 * 1024 * 1024),
        cost_estimate=pl.CostEstimate(flops=2 * macs, bytes_accessed=8 << 20, transcendentals=0),
        name="product_last" if last else "product",
    )(own, nums, *pieces, *b, *([] if first else [acc]))


def pack_kernel(stiff_ref, pos_ref, count_ref, out_ref, row_ref, *, brows):
    steps, slots, flat = stiff_ref.shape
    for s in range(steps):
        out_ref[:, s * flat : (s + 1) * flat] = stiff_ref[s]
    row_ref[...] = jnp.zeros_like(row_ref)
    for s in range(steps):
        pos = pos_ref[s : s + 1, :]
        ids = lax.broadcasted_iota(jnp.int32, pos.shape, 1)
        spot = jnp.where(ids < count_ref[s], (pos % KW) * brows + pos // KW, KW * brows)
        row_ref[s : s + 1, 0:slots] = spot.astype(jnp.float32)
    out_ref[:, steps * flat :] = row_ref[...].astype(jnp.bfloat16)


def finish_kernel(parts_ref, out_ref, rows_ref):
    total = jnp.sum(parts_ref[...], axis=0)
    for j in range(total.shape[0] // TILES):
        for h in range(2):
            rows_ref[pl.ds(j * BLK + h, TILES, stride=2), :] = total[
                j * TILES : (j + 1) * TILES, h * LANES : (h + 1) * LANES
            ]
    out_ref[...] = rows_ref[...].astype(jnp.bfloat16)


def body(stiff_blocks, block_pos, block_count, modes, panel_owner):
    layers, nx, nz = lax.axis_size("layer"), lax.axis_size("x"), lax.axis_size("zb")
    x, core, zb, zc = (lax.axis_index(a) for a in ("x", "core", "zb", "zc"))
    slots = stiff_blocks.shape[4]
    brows = slots * 2 // KW
    width = modes.shape[3]
    depth = modes.shape[2]
    blks = depth // BLK

    def turn(v, k):
        pairs = [(c * nz + i, c * nz + (i + (k if c == 0 else -k)) % nz) for c in range(2) for i in range(nz)]
        return lax.ppermute(v, ("core", "zb"), pairs)

    own_piece = pl.pallas_call(
        functools.partial(pack_kernel, brows=brows),
        out_shape=jax.ShapeDtypeStruct((slots, STEPS * FLAT + LANES), jnp.bfloat16),
        scratch_shapes=[pltpu.VMEM((slots, LANES), jnp.float32)],
        in_specs=[pl.BlockSpec(memory_space=pltpu.VMEM)] * 2 + [pl.BlockSpec(memory_space=pltpu.SMEM)],
        name="pack",
    )(stiff_blocks[0, 0, 0], block_pos[0, 0, 0], block_count[0, 0, 0])

    half = nz // 2
    fwd, back = [own_piece], [own_piece]

    def after(value, *others):
        return lax.optimization_barrier((value, *others))

    mine = modes.reshape(STEPS * depth, width)
    far = lax.ppermute(mine, "zc", [(0, 1), (1, 0)])
    fwd.append(turn(fwd[0], 1))
    back[0], far = after(back[0], far)
    mine = jnp.concatenate([mine, far], axis=0)
    moved = [lax.ppermute(mine, "x", [(i, (i - k) % nx) for i in range(nx)]) for k in range(1, nx)]
    back.append(turn(back[0], -1))
    fwd.append(turn(fwd[1], 1))
    back[1], fwd[1] = after(back[1], fwd[1])
    back.append(turn(back[1], -1))
    fwd[2], back[1], *moved = after(fwd[2], back[1], *moved)
    fwd.append(turn(fwd[2], 1))
    back[2], fwd[2] = after(back[2], fwd[2])
    back.append(turn(back[2], -1))
    mine = jnp.concatenate([mine] + moved, axis=0)
    other = lax.ppermute(mine, "core", [(0, 1), (1, 0)])
    fwd[3], back[2] = after(fwd[3], back[2])
    b = [v.reshape(-1, BLK, width) for v in (mine, other)]
    far_end = turn(fwd[3], 1)

    def number(away):
        sign = 1 - 2 * core
        return ((zb - sign * away) % nz) * GROUP + zc

    whole = lambda i: ((i, 0), (i, FLAT), (i, 2 * FLAT))
    own = panel_owner[0]
    call = functools.partial(product, brows=brows, slots=slots, blks=blks, layers=layers)

    def nums(aways):
        return jnp.stack([number(a) for a in aways] + [x, core, zc]).astype(jnp.int32)

    pieces, aways = [own_piece], [0]
    for i in range(1, half - 1):
        pieces += [fwd[i], back[i]]
        aways += [i, -i]
    acc = call(own, nums(aways), pieces, [whole(i) for i in range(len(pieces))], b, None, last=False)
    i = half - 1
    out = call(own, nums([i, -i, half]), [fwd[i], back[i], far_end], [whole(k) for k in range(3)], b, acc, last=True)
    out = lax.all_to_all(out, ("layer", "zc"), 0, 0, tiled=True)
    return pl.pallas_call(
        finish_kernel,
        out_shape=jax.ShapeDtypeStruct((brows * BLK // layers, width), jnp.bfloat16),
        scratch_shapes=[pltpu.VMEM((brows * BLK // layers, width), jnp.float32)],
        name="finish",
    )(out)


def solution(mesh):
    layers, rows, cols = (mesh.shape[a] for a in ("layer", "row", "col"))
    fine = Mesh(
        mesh.devices.reshape(layers, rows // 2, 2, cols // GROUP, GROUP), ("layer", "x", "core", "zb", "zc")
    )
    row, col = ("x", "core"), ("zb", "zc")
    return jax.shard_map(
        body,
        mesh=fine,
        in_specs=(
            P("layer", row, col, None, None, None),
            P("layer", row, col, None, None),
            P("layer", row, col, None),
            P("layer", None, row, col),
            P("layer", None, None),
        ),
        out_specs=P(row + ("layer",), col),
        check_vma=False,
    )
```
